512 devices in a mesh: seq: 128 (over z, x, y_hi), head: 4 (over y_lo, core).
Axes of the slice: x: 4, y: 4 (y_hi: 2, y_lo: 2; y = y_hi * 2 + y_lo), z: 16, core: 2. Of those that a mesh axis runs over, the one named last changes fastest.
Arguments:
- query_rows: bfloat16 [24576, 1536], P('seq', 'head'), may hold values from -64 to 64
- key_rows: bfloat16 [24576, 1536], P('seq', 'head'), may hold values from -4 to 4
- value_rows: bfloat16 [24576, 1536], P('seq', 'head'), may hold values from -6 to 6
- attention_out: bfloat16 [24576, 1536], P('seq', 'head'), may hold values from -4 to 4
- output_grad: bfloat16 [24576, 1536], P('seq', 'head'), may hold values from -6 to 6
- out_weight: bfloat16 [768, 768], P('head'), may hold values from -0.21875 to 0.21875
- reach_mask: int32 [128, 12], P('seq'), may hold values 0 or 1
Outputs:
- query_grad: bfloat16 [24576, 1536], P('seq', 'head')
- key_grad: bfloat16 [24576, 1536], P('seq', 'head')
- value_grad: bfloat16 [24576, 1536], P('seq', 'head')
The draws below stay inside these ranges and needn't reach their ends.
All inputs are finite; a program needn't handle non-finite values. No bound on the sum of `reach_mask` on one device may be relied on, other than what follows from the above.
Results may differ from the reference program's by a relative error of at most 0.017.
Values may be sent and summed in bfloat16 or wider, within the bound.
A program may use at most 128 MiB of HBM per device.

```python
import jax
import jax.numpy as jnp
from jax import lax

D = 768
HEADS = 12
HDIM = 64
LEVELS = 6
BLK = 384
REACH = 12
NBLK = 128
TOKENS = 49152


def paired_draw(key):
    base_key = jax.random.fold_in(key, 11)
    query_seed, key_seed = jax.random.split(base_key)
    array_shape = (TOKENS, HEADS * HDIM)
    query_draw = jnp.clip(jax.random.normal(query_seed, array_shape, jnp.float32), -4.0, 4.0)
    key_draw = jnp.clip(jax.random.normal(key_seed, array_shape, jnp.float32), -4.0, 4.0)
    return (query_draw, key_draw)


def pair_layout(array):
    return array.reshape(TOKENS // 2, 2, HEADS, HDIM).transpose(0, 2, 1, 3).reshape(TOKENS // 2, HEADS * 2 * HDIM)


def draw_query_rows(key, part):
    return pair_layout(paired_draw(key)[0]).astype(jnp.bfloat16)


def draw_key_rows(key, part):
    return pair_layout(paired_draw(key)[1]).astype(jnp.bfloat16)


def with_ends(entries, key, smallest, top_value):
    shape = entries.shape
    spot = [jax.random.randint(jax.random.fold_in(key, axis), (), 0, shape[axis]) for axis in range(len(shape))]
    entries = entries.at[tuple(spot)].set(smallest)
    longest = shape.index(max(shape))
    spot[longest] = (spot[longest] + 1) % shape[longest]
    return entries.at[tuple(spot)].set(top_value)


def block_scale(own_key, extent, shards, least, high):
    factor_of = 1.0
    for dim, blocks in shards:
        heights = jax.random.uniform(jax.random.fold_in(jax.random.fold_in(own_key, 6), dim), (blocks,), jnp.float32, least / len(shards), high / len(shards))
        factor_of = factor_of * jnp.repeat(jnp.exp(heights), extent[dim] // blocks).reshape((-1,) + (1,) * (len(extent) - 1 - dim))
    return factor_of


def scatter_about(stream_key, shape, deviation, bound, cuts=(), held_as=jnp.bfloat16):
    values = deviation * jax.random.normal(stream_key, shape, jnp.float32)
    if cuts:
        values = values * block_scale(stream_key, shape, cuts, -0.22, 0.18)
    return jnp.clip(values, -bound, bound).astype(held_as)


def setup_inputs(seed: int = 0) -> dict:
    streams_of = jax.random.split(jax.random.key(seed), 8)
    return {
        "query_rows": draw_query_rows(jax.random.fold_in(streams_of[7], 71), 0),
        "key_rows": draw_key_rows(jax.random.fold_in(streams_of[7], 71), 0),
        "value_rows": scatter_about(streams_of[2], (TOKENS // 2, HEADS * 2 * HDIM), 1.0, 6.0, ((0, 128), (1, 4))),
        "attention_out": scatter_about(streams_of[3], (TOKENS // 2, HEADS * 2 * HDIM), 0.5, 4.0, ((0, 128), (1, 4))),
        "output_grad": scatter_about(streams_of[4], (TOKENS // 2, 2 * D), 1.0, 6.0, ((0, 128), (1, 4))),
        "out_weight": scatter_about(streams_of[5], (HEADS * HDIM, D), D ** -0.5, 0.21875, ((0, 4),)),
        "reach_mask": with_ends((jax.random.randint(streams_of[6], (NBLK, REACH), 0, 4) < 3).astype(jnp.int32), jax.random.fold_in(streams_of[6], 1), 0, 1),
    }


def offset_list():
    result = [0]
    for exponent in range(LEVELS):
        result.append(2 ** exponent)
        result.append(-(2 ** exponent))
    return result


def from_pairs(array):
    return array.reshape(TOKENS // 2, HEADS, 2, HDIM).transpose(0, 2, 1, 3).reshape(TOKENS, HEADS * HDIM)


def to_pairs(array):
    return array.reshape(TOKENS // 2, 2, HEADS, HDIM).transpose(0, 2, 1, 3).reshape(TOKENS // 2, HEADS * 2 * HDIM)


def reference(query_rows, key_rows, value_rows, attention_out, output_grad, out_weight, reach_mask):
    scaling = HDIM ** -0.5
    offsets = offset_list()
    query_rows = from_pairs(query_rows)
    key_rows = from_pairs(key_rows)
    value_rows = from_pairs(value_rows)
    attention_out = from_pairs(attention_out)
    output_grad = output_grad.reshape(TOKENS, D)
    attn_grad = jnp.dot(output_grad, out_weight.T, preferred_element_type=jnp.float32).astype(jnp.bfloat16)
    row_delta = jnp.sum((attn_grad.astype(jnp.float32) * attention_out.astype(jnp.float32)).reshape(TOKENS, HEADS, HDIM), axis=-1)
    query_blocks = query_rows.reshape(NBLK, BLK, HEADS, HDIM)
    key_blocks = key_rows.reshape(NBLK, BLK, HEADS, HDIM)
    value_blocks = value_rows.reshape(NBLK, BLK, HEADS, HDIM)
    grad_blocks = attn_grad.reshape(NBLK, BLK, HEADS, HDIM)
    delta_blocks = row_delta.reshape(NBLK, BLK, HEADS)
    active_full = jnp.concatenate([jnp.ones((NBLK, 1), jnp.int32), reach_mask.astype(jnp.int32)], axis=1)

    def one_block(totals, block_index):
        key_total, value_total = totals
        targets = [(block_index + offset) % NBLK for offset in offsets]
        near_keys = jnp.stack([key_blocks[target] for target in targets]).astype(jnp.float32)
        near_values = jnp.stack([value_blocks[target] for target in targets]).astype(jnp.float32)
        queries_here = query_blocks[block_index].astype(jnp.float32)
        grads_here = grad_blocks[block_index].astype(jnp.float32)
        delta_here = delta_blocks[block_index]
        live_mask = (active_full[block_index] > 0)[None, None, :, None]
        scores = jnp.einsum('qhd,ckhd->hqck', queries_here, near_keys) * scaling
        masked = jnp.where(live_mask, scores, -1e30)
        row_max = jnp.max(masked, axis=(2, 3))
        row_sum = jnp.sum(jnp.exp(masked - row_max[:, :, None, None]), axis=(2, 3))
        log_total = row_max + jnp.log(row_sum)
        prob_full = jnp.where(live_mask, jnp.exp(scores - log_total[:, :, None, None]), 0.0)
        prob_half = prob_full.astype(jnp.bfloat16)
        prob_grad = jnp.einsum('qhd,ckhd->hqck', grads_here, near_values)
        score_grad = (prob_full * (prob_grad - delta_here.T[:, :, None, None]) * scaling).astype(jnp.bfloat16)
        score_wide = score_grad.astype(jnp.float32)
        query_grad = jnp.einsum('hqck,ckhd->qhd', score_wide, near_keys)
        key_part = jnp.einsum('hqck,qhd->ckhd', score_wide, queries_here)
        value_part = jnp.einsum('hqck,qhd->ckhd', prob_half.astype(jnp.float32), grads_here)
        for column, target in enumerate(targets):
            key_total = key_total.at[target].add(key_part[column])
            value_total = value_total.at[target].add(value_part[column])
        return (key_total, value_total), query_grad

    zero_blocks = jnp.zeros((NBLK, BLK, HEADS, HDIM), jnp.float32)
    (key_total, value_total), query_grads = lax.scan(one_block, (zero_blocks, zero_blocks), jnp.arange(NBLK, dtype=jnp.int32))
    query_grad = to_pairs(query_grads.reshape(TOKENS, HEADS * HDIM)).astype(jnp.bfloat16)
    key_grad = to_pairs(key_total.reshape(TOKENS, HEADS * HDIM)).astype(jnp.bfloat16)
    value_grad = to_pairs(value_total.reshape(TOKENS, HEADS * HDIM)).astype(jnp.bfloat16)
    return (query_grad, key_grad, value_grad)
```

```python
import jax
import jax.numpy as jnp
from jax import lax
from jax.experimental import pallas as pl
from jax.experimental.pallas import tpu as pltpu
from jax.sharding import PartitionSpec as P

MESH = pl.DeviceIdType.MESH
HDIM = 64
PLANE = 8
SLOTS = 13
DELTA = (0, -8, 8, -16, 16, -1, 1, -2, 2, -4, 4, -32, 32)
SCALING = HDIM**-0.5
EXP2_SCALE = SCALING * 1.4426950408889634
F32 = jnp.float32
BF16 = jnp.bfloat16


def mask_column(delta):
    return 2 * (abs(delta).bit_length() - 1) + (delta < 0)


def opposite(slot):
    return slot + 1 - 2 * ((slot + 1) % 2)


def slot_delta(slot):
    pair = (slot + 1) // 2
    power = (pair + 2) % 5 + 2 * (pair // 6)
    size = (1 + power % 2) * (1 + 3 * ((power // 2) % 2)) * (1 + 15 * (power // 4))
    return size * (1 - 2 * (slot % 2))


def dot_nt(left, right):
    return lax.dot_general(left, right, (((1,), (1,)), ((), ())), preferred_element_type=F32)


def dot_nn(left, right):
    return jnp.dot(left, right, preferred_element_type=F32)


def kernel(
    blocks,
    heads,
    q_ref,
    k_ref,
    v_ref,
    ao_ref,
    og_ref,
    w_ref,
    reach_ref,
    dq_ref,
    dk_ref,
    dv_ref,
    qbuf,
    gbuf,
    ogbuf,
    wide,
    ebuf,
    kfull,
    vfull,
    ktrans,
    delta_rows,
    stat_out,
    stat_in,
    fact_out,
    fact_in,
    part_out,
    part_in,
    dk_acc,
    dv_acc,
    dq_acc,
    q_send,
    q_recv,
    g_send,
    g_recv,
    og_send,
    og_recv,
    stat_send,
    stat_recv,
    fact_send,
    fact_recv,
    part_send,
    part_recv,
):
    pairs, width = q_ref.shape
    head_count = width // (2 * HDIM)
    me = lax.axis_index("seq")
    my_head = lax.axis_index("head")
    spot = lax.rem(me, PLANE)
    plane_start = me - spot

    def at(delta):
        return lax.rem(me + delta + blocks, blocks)

    def in_plane(delta):
        return plane_start + lax.rem(spot + delta + PLANE, PLANE)

    def head_at(step):
        return lax.rem(my_head + step, heads)

    barrier = pltpu.get_barrier_semaphore()
    for delta in DELTA[1:]:
        pl.semaphore_signal(barrier, inc=1, device_id=(at(delta), my_head), device_id_type=MESH)
    for delta in (-1, 1, -2, 2, 4):
        pl.semaphore_signal(barrier, inc=1, device_id=(in_plane(delta), my_head), device_id_type=MESH)
    for step in range(1, heads):
        pl.semaphore_signal(barrier, inc=1, device_id=(me, head_at(step)), device_id_type=MESH)

    lane = lax.broadcasted_iota(jnp.int32, (1, 2 * HDIM), 1)
    low = lane < HDIM
    low_f = low.astype(F32)
    low_b = low_f.astype(BF16)
    high_b = (1.0 - low_f).astype(BF16)

    def cols(head):
        return pl.ds(head * 2 * HDIM, 2 * HDIM)

    def doubled(tile):
        tile = tile.astype(F32)
        turned = pltpu.roll(tile, HDIM, 1)
        return jnp.concatenate([jnp.where(low, tile, turned), jnp.where(low, turned, tile)], axis=0)

    def spread(tile):
        return jnp.concatenate([tile * low_b, tile * high_b], axis=0)

    qbuf[0] = q_ref[...]
    ogbuf[my_head] = og_ref[...]

    pl.semaphore_wait(barrier, 17 + heads - 1)

    def remote(src, dst, send_sem, recv_sem, seq, head=None):
        return pltpu.make_async_remote_copy(
            src_ref=src,
            dst_ref=dst,
            send_sem=send_sem,
            recv_sem=recv_sem,
            device_id=(seq, my_head if head is None else head),
            device_id_type=MESH,
        )

    def move(buf, send, recv, src_slot, dst_slot, seq):
        return remote(buf.at[src_slot], buf.at[dst_slot], send.at[dst_slot], recv.at[dst_slot], seq)

    def slot_of(delta):
        return DELTA.index(delta)

    def send_own(buf, send, recv):
        move(buf, send, recv, 0, slot_of(-8), at(8)).start()
        move(buf, send, recv, 0, slot_of(8), at(-8)).start()

    def send_plane_own(buf, send, recv):
        for delta in (4, -4, 2, -2, 1, -1):
            inside = spot + delta < PLANE if delta > 0 else spot + delta >= 0

            @pl.when(inside)
            def _():
                move(buf, send, recv, 0, slot_of(-delta), in_plane(delta)).start()

    def relay_near(buf, send, recv, sign):
        source = slot_of(-8 * sign)
        move(buf, send, recv, source, slot_of(-16 * sign), at(8 * sign)).start()
        for size in (4, 2, 1):
            delta = size * sign
            inside = spot + delta < PLANE if delta > 0 else spot + delta >= 0

            @pl.when(jnp.logical_not(inside))
            def _():
                move(buf, send, recv, source, slot_of(-delta), in_plane(delta)).start()

    def relay_far(buf, send, recv, sign):
        move(buf, send, recv, slot_of(-16 * sign), slot_of(-32 * sign), at(16 * sign)).start()

    def wait_recv(buf, send, recv, slot):
        move(buf, send, recv, slot, slot, at(8)).wait_recv()

    def wait_send(buf, send, recv, slot):
        move(buf, send, recv, slot, slot, at(8)).wait_send()

    send_own(qbuf, q_send, q_recv)
    for step in range(1, heads):
        remote(
            ogbuf.at[my_head], ogbuf.at[my_head], og_send.at[step], og_recv.at[my_head], me, head_at(step)
        ).start()
    send_plane_own(qbuf, q_send, q_recv)

    for head in range(head_count):
        keys = doubled(k_ref[:, cols(head)])
        kfull[head] = keys.astype(BF16)
        ktrans[head] = jnp.transpose(keys)[:HDIM].astype(BF16)
        vfull[head] = doubled(v_ref[:, cols(head)]).astype(BF16)
        dk_acc[head] = jnp.zeros((2 * pairs, 2 * HDIM), F32)
        dv_acc[head] = jnp.zeros((2 * pairs, 2 * HDIM), F32)
    wide[...] = jnp.zeros(wide.shape, BF16)
    for head in range(head_count):
        rows = w_ref[pl.ds(head * HDIM, HDIM), :]
        for parity in range(2):
            wide[parity, pl.ds((head * 2 + parity) * HDIM, HDIM), :] = rows

    def grads_of_attention():
        for step in range(1, heads):
            other = head_at(step)
            remote(ogbuf.at[other], ogbuf.at[other], og_send.at[step], og_recv.at[other], me, other).wait_recv()
        total = jnp.zeros((pairs, width), F32)
        for chunk in range(heads):
            half = chunk % 2
            total = total + dot_nt(ogbuf[chunk], wide[chunk // 2, :, pl.ds(half * width, width)])
        grads = total.astype(BF16)
        gbuf[0] = grads
        product = grads.astype(F32) * ao_ref[...].astype(F32)
        column = lax.broadcasted_iota(jnp.int32, (1, width), 1)
        first = lax.rem(column, 2 * HDIM) < HDIM
        both = jnp.concatenate([jnp.where(first, product, 0.0), jnp.where(first, 0.0, product)], axis=0)
        top = both.astype(BF16)
        rest = (both - top.astype(F32)).astype(BF16)
        chooser = (
            lax.broadcasted_iota(jnp.int32, (8, width), 1) // (2 * HDIM)
            == lax.broadcasted_iota(jnp.int32, (8, width), 0)
        )
        chooser = chooser.astype(F32).astype(BF16)
        delta_rows[...] = dot_nt(chooser, top) + dot_nt(chooser, rest)

    def first_pass(slot, carry):
        @pl.when(slot > 0)
        def _():
            wait_recv(qbuf, q_send, q_recv, slot)

        for sign in (1, -1):

            @pl.when(slot == slot_of(-8 * sign))
            def _():
                relay_near(qbuf, q_send, q_recv, sign)

            @pl.when(slot == slot_of(-16 * sign))
            def _():
                relay_far(qbuf, q_send, q_recv, sign)

        @pl.when(slot == 5)
        def _():
            grads_of_attention()
            send_own(gbuf, g_send, g_recv)
            send_plane_own(gbuf, g_send, g_recv)

        tops, sums = [], []
        for head in range(head_count):
            queries = spread(qbuf[slot, :, cols(head)])
            scores = dot_nt(kfull[head], queries)
            top = jnp.max(scores, axis=0, keepdims=True)
            weights = jnp.exp2((scores - top) * EXP2_SCALE)
            tops.append(top)
            sums.append(jnp.sum(weights, axis=0, keepdims=True))
            ebuf[slot * head_count + head] = weights.astype(BF16)
        stat_out[slot] = jnp.concatenate(tops + tops[:1] + sums + sums[:1], axis=0)

        @pl.when(slot > 0)
        def _():
            there = opposite(slot)
            remote(
                stat_out.at[slot],
                stat_in.at[there],
                stat_send.at[slot],
                stat_recv.at[there],
                at(slot_delta(slot)),
            ).start()

        return carry

    lax.fori_loop(0, SLOTS, first_pass, 0)

    for sign in (1, -1):
        wait_recv(gbuf, g_send, g_recv, slot_of(-8 * sign))
        relay_near(gbuf, g_send, g_recv, sign)

    live = [None] + [reach_ref[0, mask_column(delta)] > 0 for delta in DELTA[1:]]
    for slot in range(1, SLOTS):
        wait_recv(stat_in, stat_send, stat_recv, slot)

    def stats(slot):
        both = stat_out[0] if slot == 0 else stat_in[slot]
        return both[0:4], both[4:8]

    highest = stats(0)[0]
    for slot in range(1, SLOTS):
        highest = jnp.maximum(highest, jnp.where(live[slot], stats(slot)[0], -1e30))
    ratios = []
    total = jnp.zeros(highest.shape, F32)
    for slot in range(SLOTS):
        top, part = stats(slot)
        ratio = jnp.exp2((top - highest) * EXP2_SCALE)
        if slot:
            ratio = jnp.where(live[slot], ratio, 0.0)
        total = total + ratio * part
        ratios.append(ratio)
    inverse = 1.0 / total
    deltas = delta_rows[0:4]
    for slot in range(SLOTS):
        factors = jnp.concatenate([ratios[slot] * inverse, deltas], axis=0)
        if slot == 0:
            fact_in[0] = factors
        else:
            fact_out[slot] = factors
            there = opposite(slot)
            remote(
                fact_out.at[slot], fact_in.at[there], fact_send.at[slot], fact_recv.at[there], at(DELTA[slot])
            ).start()

    for sign in (1, -1):
        wait_recv(gbuf, g_send, g_recv, slot_of(-16 * sign))
        relay_far(gbuf, g_send, g_recv, sign)

    def second_pass(slot, carry):
        @pl.when(jnp.logical_or(slot == 0, slot > 4))
        def _():
            @pl.when(slot > 0)
            def _():
                wait_recv(gbuf, g_send, g_recv, slot)

        @pl.when(slot > 0)
        def _():
            wait_recv(fact_in, fact_send, fact_recv, slot)

        for head in range(head_count):
            queries = spread(qbuf[slot, :, cols(head)])
            grads = spread(gbuf[slot, :, cols(head)])
            factor = fact_in[slot, pl.ds(head, 1), :]
            shift = fact_in[slot, pl.ds(4 + head, 1), :]
            prob_grad = dot_nt(vfull[head], grads)
            prob = ebuf[slot * head_count + head].astype(F32) * factor
            score_grad = (prob * (prob_grad - shift)).astype(BF16)
            dv_acc[head] += dot_nn(prob.astype(BF16), grads)
            dk_acc[head] += dot_nn(score_grad, queries)
            part_out[slot, pl.ds(head * HDIM, HDIM), :] = dot_nn(ktrans[head], score_grad).astype(BF16)

        @pl.when(slot > 0)
        def _():
            there = opposite(slot)
            remote(
                part_out.at[slot],
                part_in.at[there],
                part_send.at[slot],
                part_recv.at[there],
                at(slot_delta(slot)),
            ).start()

        return carry

    lax.fori_loop(0, SLOTS, second_pass, 0)

    def folded(wide_sum):
        both = wide_sum + pltpu.roll(wide_sum, HDIM, 1)
        return jnp.where(low, both[:pairs], both[pairs:])

    for head in range(head_count):
        dk_ref[:, cols(head)] = (folded(dk_acc[head]) * SCALING).astype(BF16)
        dv_ref[:, cols(head)] = folded(dv_acc[head]).astype(BF16)

    dq_acc[...] = part_out[0].astype(F32)

    def gather_part(slot, carry):
        wait_recv(part_in, part_send, part_recv, slot)
        dq_acc[...] += part_in[slot].astype(F32)
        return carry

    lax.fori_loop(1, SLOTS, gather_part, 0)
    for head in range(head_count):
        rows = dq_acc[pl.ds(head * HDIM, HDIM), :] * SCALING
        turned = jnp.transpose(jnp.concatenate([rows, rows], axis=0))
        dq_ref[:, cols(head)] = jnp.where(low, turned[:pairs], turned[pairs:]).astype(BF16)

    for step in range(1, heads):
        remote(
            ogbuf.at[my_head], ogbuf.at[my_head], og_send.at[step], og_recv.at[my_head], me, head_at(step)
        ).wait_send()

    def drain(slot, carry):
        wait_send(qbuf, q_send, q_recv, slot)
        wait_send(gbuf, g_send, g_recv, slot)
        wait_send(stat_in, stat_send, stat_recv, slot)
        wait_send(fact_in, fact_send, fact_recv, slot)
        wait_send(part_in, part_send, part_recv, slot)
        return carry

    lax.fori_loop(1, SLOTS, drain, 0)


def solution(mesh):
    blocks, heads = mesh.shape["seq"], mesh.shape["head"]

    def step(query_rows, key_rows, value_rows, attention_out, output_grad, out_weight, reach_mask):
        pairs, width = query_rows.shape
        head_count = width // (2 * HDIM)
        tokens = 2 * pairs
        vmem = pl.BlockSpec(memory_space=pltpu.VMEM)
        block = jax.ShapeDtypeStruct((pairs, width), BF16)
        dma = pltpu.SemaphoreType.DMA

        def body(*refs):
            kernel(blocks, heads, *refs)

        return pl.pallas_call(
            body,
            out_shape=(block, block, block),
            in_specs=[vmem] * 6 + [pl.BlockSpec(memory_space=pltpu.SMEM)],
            out_specs=(vmem, vmem, vmem),
            scratch_shapes=[
                pltpu.VMEM((SLOTS, pairs, width), BF16),
                pltpu.VMEM((SLOTS, pairs, width), BF16),
                pltpu.VMEM((heads, pairs, width), BF16),
                pltpu.VMEM((2, width, out_weight.shape[1]), BF16),
                pltpu.VMEM((SLOTS * head_count, tokens, tokens), BF16),
                pltpu.VMEM((head_count, tokens, 2 * HDIM), BF16),
                pltpu.VMEM((head_count, tokens, 2 * HDIM), BF16),
                pltpu.VMEM((head_count, HDIM, tokens), BF16),
                pltpu.VMEM((8, tokens), F32),
                pltpu.VMEM((SLOTS, 8, tokens), F32),
                pltpu.VMEM((SLOTS, 8, tokens), F32),
                pltpu.VMEM((SLOTS, 8, tokens), F32),
                pltpu.VMEM((SLOTS, 8, tokens), F32),
                pltpu.VMEM((SLOTS, head_count * HDIM, tokens), BF16),
                pltpu.VMEM((SLOTS, head_count * HDIM, tokens), BF16),
                pltpu.VMEM((head_count, tokens, 2 * HDIM), F32),
                pltpu.VMEM((head_count, tokens, 2 * HDIM), F32),
                pltpu.VMEM((head_count * HDIM, tokens), F32),
                dma((SLOTS,)),
                dma((SLOTS,)),
                dma((SLOTS,)),
                dma((SLOTS,)),
                dma((heads,)),
                dma((heads,)),
                dma((SLOTS,)),
                dma((SLOTS,)),
                dma((SLOTS,)),
                dma((SLOTS,)),
                dma((SLOTS,)),
                dma((SLOTS,)),
            ],
            compiler_params=pltpu.CompilerParams(
                collective_id=0, has_side_effects=True, vmem_limit_bytes=52 * 1024 * 1024
            ),
            cost_estimate=pl.CostEstimate(flops=8 * 10**9, bytes_accessed=2 * 10**6, transcendentals=6 * 10**6),
        )(query_rows, key_rows, value_rows, attention_out, output_grad, out_weight, reach_mask)

    rows = P("seq", "head")
    return jax.shard_map(
        step,
        mesh=mesh,
        in_specs=(rows, rows, rows, rows, rows, P("head", None), P("seq", None)),
        out_specs=(rows, rows, rows),
        check_vma=False,
    )
```

```python
import jax
import jax.numpy as jnp
from jax import lax
from jax.experimental import pallas as pl
from jax.experimental.pallas import tpu as pltpu
from jax.sharding import PartitionSpec as P

MESH = pl.DeviceIdType.MESH
HDIM = 64
PLANE = 8
SLOTS = 13
DELTA = (0, -8, 8, -16, 16, -1, 1, -2, 2, -4, 4, -32, 32)
SCALING = HDIM**-0.5
EXP2_SCALE = SCALING * 1.4426950408889634
F32 = jnp.float32
BF16 = jnp.bfloat16


def mask_column(delta):
    return 2 * (abs(delta).bit_length() - 1) + (delta < 0)


def opposite(slot):
    return slot + 1 - 2 * ((slot + 1) % 2)


def slot_delta(slot):
    pair = (slot + 1) // 2
    power = (pair + 2) % 5 + 2 * (pair // 6)
    size = (1 + power % 2) * (1 + 3 * ((power // 2) % 2)) * (1 + 15 * (power // 4))
    return size * (1 - 2 * (slot % 2))


def dot_nt(left, right):
    return lax.dot_general(left, right, (((1,), (1,)), ((), ())), preferred_element_type=F32)


def dot_nn(left, right):
    return jnp.dot(left, right, preferred_element_type=F32)


TAIL = 16


def kernel(
    blocks,
    heads,
    q_hbm,
    k_hbm,
    v_hbm,
    ao_hbm,
    og_hbm,
    w_hbm,
    reach_hbm,
    dq_ref,
    dk_ref,
    dv_ref,
    k_ref,
    v_ref,
    ao_ref,
    w_ref,
    reach_ref,
    qbuf,
    gbuf,
    ogbuf,
    wide,
    ebuf,
    ubuf,
    kfull,
    vfull,
    ktrans,
    stat_out,
    stat_in,
    fact_out,
    fact_in,
    dq_raw,
    part_out,
    part_in,
    dk_acc,
    dv_acc,
    dq_acc,
    local_sem,
    q_send,
    q_recv,
    g_send,
    g_recv,
    og_send,
    og_recv,
    stat_send,
    stat_recv,
    fact_send,
    fact_recv,
    part_send,
    part_recv,
):
    _, pairs, width = qbuf.shape
    head_count = width // (2 * HDIM)
    me = lax.axis_index("seq")
    my_head = lax.axis_index("head")
    spot = lax.rem(me, PLANE)
    plane_start = me - spot

    def at(delta):
        return lax.rem(me + delta + blocks, blocks)

    def in_plane(delta):
        return plane_start + lax.rem(spot + delta + PLANE, PLANE)

    def stays(delta):
        return spot + delta < PLANE if delta > 0 else spot + delta >= 0

    def head_at(step):
        return lax.rem(my_head + step, heads)

    barrier = pltpu.get_barrier_semaphore()
    for delta in DELTA[1:]:
        pl.semaphore_signal(barrier, inc=1, device_id=(at(delta), my_head), device_id_type=MESH)
    for delta in (-1, 1, -2, 2, 4):
        pl.semaphore_signal(barrier, inc=1, device_id=(in_plane(delta), my_head), device_id_type=MESH)
    for step in range(1, heads):
        pl.semaphore_signal(barrier, inc=1, device_id=(me, head_at(step)), device_id_type=MESH)

    loads = [
        pltpu.make_async_copy(src, dst, local_sem.at[i])
        for i, (src, dst) in enumerate(
            [
                (k_hbm, k_ref),
                (q_hbm, qbuf.at[0]),
                (v_hbm, v_ref),
                (w_hbm, w_ref),
                (ao_hbm, ao_ref),
                (og_hbm, ogbuf.at[my_head]),
                (reach_hbm, reach_ref),
            ]
        )
    ]
    for load in loads:
        load.start()

    lane = lax.broadcasted_iota(jnp.int32, (1, 2 * HDIM), 1)
    low = lane < HDIM
    low_f = low.astype(F32)
    low_b = low_f.astype(BF16)
    high_b = (1.0 - low_f).astype(BF16)

    def cols(head):
        return pl.ds(head * 2 * HDIM, 2 * HDIM)

    def head_rows(head):
        return pl.ds(head * HDIM, HDIM)

    def doubled(tile):
        tile = tile.astype(F32)
        turned = pltpu.roll(tile, HDIM, 1)
        return jnp.concatenate([jnp.where(low, tile, turned), jnp.where(low, turned, tile)], axis=0)

    def spread(tile):
        return jnp.concatenate([tile * low_b, tile * high_b], axis=0)

    pl.semaphore_wait(barrier, 17 + heads - 1)

    def remote(src, dst, send_sem, recv_sem, seq, head=None):
        return pltpu.make_async_remote_copy(
            src_ref=src,
            dst_ref=dst,
            send_sem=send_sem,
            recv_sem=recv_sem,
            device_id=(seq, my_head if head is None else head),
            device_id_type=MESH,
        )

    queries_net = (qbuf, q_send, q_recv)
    grads_net = (gbuf, g_send, g_recv)
    stats_net = (stat_in, stat_send, stat_recv)
    facts_net = (fact_in, fact_send, fact_recv)
    parts_net = (part_in, part_send, part_recv)

    def move(net, src, dst_slot, seq):
        buf, send, recv = net
        return remote(src, buf.at[dst_slot], send.at[dst_slot], recv.at[dst_slot], seq)

    def wait_recv(net, slot):
        move(net, net[0].at[slot], slot, at(8)).wait_recv()

    def wait_send(net, slot):
        move(net, net[0].at[slot], slot, at(8)).wait_send()

    def slot_of(delta):
        return DELTA.index(delta)

    def send_own(net, src):
        for sign in (1, -1):
            move(net, src, slot_of(-8 * sign), at(8 * sign)).start()

    def send_plane_own(net, src):
        for delta in (4, -4, 2, -2, 1, -1):

            @pl.when(stays(delta))
            def _():
                move(net, src, slot_of(-delta), in_plane(delta)).start()

    def relay_near(net, sign):
        source = net[0].at[slot_of(-8 * sign)]
        move(net, source, slot_of(-16 * sign), at(8 * sign)).start()
        for size in (4, 2, 1):
            delta = size * sign

            @pl.when(jnp.logical_not(stays(delta)))
            def _():
                move(net, source, slot_of(-delta), in_plane(delta)).start()

    def relay_far(net, sign):
        move(net, net[0].at[slot_of(-16 * sign)], slot_of(-32 * sign), at(16 * sign)).start()

    send_own(queries_net, q_hbm)
    for step in range(1, heads):
        remote(og_hbm, ogbuf.at[my_head], og_send.at[step], og_recv.at[my_head], me, head_at(step)).start()
    send_plane_own(queries_net, q_hbm)

    for load in loads:
        load.wait()
    for head in range(head_count):
        keys = doubled(k_ref[:, cols(head)])
        kfull[head] = keys.astype(BF16)
        ktrans[head] = jnp.transpose(keys)[:HDIM].astype(BF16)
        vfull[head] = doubled(v_ref[:, cols(head)]).astype(BF16)
        dk_acc[head] = jnp.zeros((2 * pairs, 2 * HDIM), F32)
        dv_acc[head] = jnp.zeros((2 * pairs, 2 * HDIM), F32)
    wide[...] = jnp.zeros(wide.shape, BF16)
    for head in range(head_count):
        rows = w_ref[pl.ds(head * HDIM, HDIM), :]
        for parity in range(2):
            wide[parity, pl.ds((head * 2 + parity) * HDIM, HDIM), :] = rows

    def grads_of_attention():
        for step in range(1, heads):
            other = head_at(step)
            remote(og_hbm, ogbuf.at[other], og_send.at[step], og_recv.at[other], me, other).wait_recv()
        total = jnp.zeros((pairs, width), F32)
        for chunk in range(heads):
            half = chunk % 2
            total = total + dot_nt(ogbuf[chunk], wide[chunk // 2, :, pl.ds(half * width, width)])
        grads = total.astype(BF16)
        gbuf[0, :pairs, :] = grads
        product = grads.astype(F32) * ao_ref[...].astype(F32)
        column = lax.broadcasted_iota(jnp.int32, (1, width), 1)
        first = lax.rem(column, 2 * HDIM) < HDIM
        both = jnp.concatenate([jnp.where(first, product, 0.0), jnp.where(first, 0.0, product)], axis=0)
        top = both.astype(BF16)
        rest = (both - top.astype(F32)).astype(BF16)
        chooser = (
            lax.broadcasted_iota(jnp.int32, (8, width), 1) // (2 * HDIM)
            == lax.broadcasted_iota(jnp.int32, (8, width), 0)
        )
        chooser = chooser.astype(F32).astype(BF16)
        delta = dot_nt(chooser, top) + dot_nt(chooser, rest)
        delta_top = delta.astype(BF16)
        delta_rest = (delta - delta_top.astype(F32)).astype(BF16)
        gbuf[0, pairs:, :] = jnp.concatenate([delta_top, delta_rest], axis=0)

    def first_pass(slot, carry):
        @pl.when(slot > 0)
        def _():
            wait_recv(queries_net, slot)

        for sign in (1, -1):

            @pl.when(slot == slot_of(-8 * sign))
            def _():
                relay_near(queries_net, sign)

            @pl.when(slot == slot_of(-16 * sign))
            def _():
                relay_far(queries_net, sign)

        @pl.when(slot == 5)
        def _():
            grads_of_attention()
            send_own(grads_net, gbuf.at[0])
            send_plane_own(grads_net, gbuf.at[0])

        tops, sums = [], []
        for head in range(head_count):
            queries = spread(qbuf[slot, :, cols(head)])
            scores = dot_nt(kfull[head], queries)
            top = jnp.max(scores, axis=0, keepdims=True)
            weights = jnp.exp2((scores - top) * EXP2_SCALE)
            tops.append(top)
            sums.append(jnp.sum(weights, axis=0, keepdims=True))
            ebuf[slot * head_count + head] = weights.astype(BF16)
        stat_out[slot] = jnp.concatenate(tops + tops[:1] + sums + sums[:1], axis=0)

        @pl.when(slot > 0)
        def _():
            there = opposite(slot)
            remote(
                stat_out.at[slot], stat_in.at[there], stat_send.at[slot], stat_recv.at[there], at(slot_delta(slot))
            ).start()

        return carry

    lax.fori_loop(0, SLOTS, first_pass, 0)

    for sign in (1, -1):
        wait_recv(grads_net, slot_of(-8 * sign))
        relay_near(grads_net, sign)

    def share_factors():
        live = [None] + [reach_ref[0, mask_column(delta)] > 0 for delta in DELTA[1:]]
        for slot in range(1, SLOTS):
            wait_recv(stats_net, slot)

        def stats(slot):
            both = stat_out[0] if slot == 0 else stat_in[slot]
            return both[0:4], both[4:8]

        highest = stats(0)[0]
        for slot in range(1, SLOTS):
            highest = jnp.maximum(highest, jnp.where(live[slot], stats(slot)[0], -1e30))
        ratios = []
        total = jnp.zeros(highest.shape, F32)
        for slot in range(SLOTS):
            top, part = stats(slot)
            if slot:
                top = jnp.where(live[slot], top, -1e30)
            ratio = jnp.exp2((top - highest) * EXP2_SCALE)
            if slot:
                ratio = jnp.where(live[slot], ratio, 0.0)
            total = total + ratio * part
            ratios.append(ratio)
        inverse = 1.0 / total
        for slot in range(SLOTS):
            factors = ratios[slot] * inverse
            factors = jnp.concatenate([factors, factors], axis=0)
            if slot == 0:
                fact_in[0] = factors
            else:
                fact_out[slot] = factors
                there = opposite(slot)
                remote(
                    fact_out.at[slot], fact_in.at[there], fact_send.at[slot], fact_recv.at[there], at(DELTA[slot])
                ).start()

    def scaled(slot):
        factors = fact_in[slot]
        return jnp.concatenate(
            [dq_raw[slot, head_rows(head), :] * factors[head : head + 1] for head in range(head_count)], axis=0
        )

    def return_part(slot, seq):
        part_out[slot] = scaled(slot).astype(BF16)
        move(parts_net, part_out.at[slot], slot, seq).start()

    def second_pass(slot, carry):
        @pl.when(slot == 3)
        def _():
            for sign in (1, -1):
                wait_recv(grads_net, slot_of(-16 * sign))
                relay_far(grads_net, sign)
            share_factors()

        @pl.when(slot == 11)
        def _():
            for delta in (4, -4, 2, -2, 1, -1):
                wait_recv(facts_net, slot_of(delta))
                return_part(slot_of(delta), in_plane(delta))

        @pl.when(slot > 4)
        def _():
            wait_recv(grads_net, slot)

        tail = gbuf[slot, pairs:, :].astype(F32)
        for head in range(head_count):
            grads = spread(gbuf[slot, :pairs, cols(head)])
            shift = tail[head : head + 1] + tail[8 + head : 9 + head]
            prob_grad = dot_nt(vfull[head], grads)
            weights = ebuf[slot * head_count + head].astype(F32)
            raw = (weights * (prob_grad - shift)).astype(BF16)
            ubuf[slot * head_count + head] = raw
            dq_raw[slot, head_rows(head), :] = dot_nn(ktrans[head], raw)
        return carry

    lax.fori_loop(0, SLOTS, second_pass, 0)

    for sign in (1, -1):
        slot = slot_of(-32 * sign)
        wait_recv(facts_net, slot)
        return_part(slot, at(-16 * sign))
    for slot in (1, 2, 3, 4):
        wait_recv(facts_net, slot)
    for slot in (0, 1, 2):
        dq_acc[slot] = scaled(slot)

    def third_pass(slot, carry):
        factors = fact_in[slot]
        for head in range(head_count):
            factor = factors[head : head + 1]
            queries = spread(qbuf[slot, :, cols(head)])
            grads = spread(gbuf[slot, :pairs, cols(head)])
            prob = (ebuf[slot * head_count + head].astype(F32) * factor).astype(BF16)
            score_grad = (ubuf[slot * head_count + head].astype(F32) * factor).astype(BF16)
            dv_acc[head] += dot_nn(prob, grads)
            dk_acc[head] += dot_nn(score_grad, queries)
        return carry

    lax.fori_loop(0, SLOTS, third_pass, 0)

    for sign in (1, -1):
        far, near = slot_of(-32 * sign), slot_of(-16 * sign)
        wait_recv(parts_net, far)
        part_out[near] = (scaled(near) + part_in[far].astype(F32)).astype(BF16)
        move(parts_net, part_out.at[near], near, at(-8 * sign)).start()

    for delta in (4, -4, 2, -2, 1, -1):
        slot = slot_of(-delta)
        owner = jnp.where(stays(delta), 0, slot_of(-8) if delta > 0 else slot_of(8))
        wait_recv(parts_net, slot)
        dq_acc[owner] += part_in[slot].astype(F32)

    def folded(wide_sum):
        both = wide_sum + pltpu.roll(wide_sum, HDIM, 1)
        return jnp.where(low, both[:pairs], both[pairs:])

    for head in range(head_count):
        dk_ref[:, cols(head)] = (folded(dk_acc[head]) * SCALING).astype(BF16)
        dv_ref[:, cols(head)] = folded(dv_acc[head]).astype(BF16)

    for sign in (1, -1):
        near, next_to = slot_of(-16 * sign), slot_of(-8 * sign)
        wait_recv(parts_net, near)
        part_out[next_to] = (dq_acc[next_to] + part_in[near].astype(F32)).astype(BF16)
        move(parts_net, part_out.at[next_to], next_to, at(-8 * sign)).start()

    for sign in (1, -1):
        slot = slot_of(-8 * sign)
        wait_recv(parts_net, slot)
    total = (dq_acc[0] + part_in[1].astype(F32) + part_in[2].astype(F32)) * SCALING
    for head in range(head_count):
        rows = total[head * HDIM : (head + 1) * HDIM]
        turned = jnp.transpose(jnp.concatenate([rows, rows], axis=0))
        dq_ref[:, cols(head)] = jnp.where(low, turned[:pairs], turned[pairs:]).astype(BF16)

    for step in range(1, heads):
        remote(og_hbm, ogbuf.at[my_head], og_send.at[step], og_recv.at[my_head], me, head_at(step)).wait_send()

    def drain(slot, carry):
        for net in (queries_net, grads_net, stats_net, facts_net, parts_net):
            wait_send(net, slot)
        return carry

    lax.fori_loop(1, SLOTS, drain, 0)


def solution(mesh):
    blocks, heads = mesh.shape["seq"], mesh.shape["head"]

    def step(query_rows, key_rows, value_rows, attention_out, output_grad, out_weight, reach_mask):
        pairs, width = query_rows.shape
        head_count = width // (2 * HDIM)
        tokens = 2 * pairs
        vmem = pl.BlockSpec(memory_space=pltpu.VMEM)
        block = jax.ShapeDtypeStruct((pairs, width), BF16)
        dma = pltpu.SemaphoreType.DMA

        def body(*refs):
            kernel(blocks, heads, *refs)

        return pl.pallas_call(
            body,
            out_shape=(block, block, block),
            in_specs=[pl.BlockSpec(memory_space=pltpu.HBM)] * 7,
            out_specs=(vmem, vmem, vmem),
            scratch_shapes=[
                pltpu.VMEM((pairs, width), BF16),
                pltpu.VMEM((pairs, width), BF16),
                pltpu.VMEM((pairs, width), BF16),
                pltpu.VMEM(out_weight.shape, BF16),
                pltpu.SMEM(reach_mask.shape, jnp.int32),
                pltpu.VMEM((SLOTS, pairs, width), BF16),
                pltpu.VMEM((SLOTS, pairs + TAIL, width), BF16),
                pltpu.VMEM((heads, pairs, width), BF16),
                pltpu.VMEM((2, width, out_weight.shape[1]), BF16),
                pltpu.VMEM((SLOTS * head_count, tokens, tokens), BF16),
                pltpu.VMEM((SLOTS * head_count, tokens, tokens), BF16),
                pltpu.VMEM((head_count, tokens, 2 * HDIM), BF16),
                pltpu.VMEM((head_count, tokens, 2 * HDIM), BF16),
                pltpu.VMEM((head_count, HDIM, tokens), BF16),
                pltpu.VMEM((SLOTS, 8, tokens), F32),
                pltpu.VMEM((SLOTS, 8, tokens), F32),
                pltpu.VMEM((SLOTS, 8, tokens), F32),
                pltpu.VMEM((SLOTS, 8, tokens), F32),
                pltpu.VMEM((SLOTS, head_count * HDIM, tokens), F32),
                pltpu.VMEM((SLOTS, head_count * HDIM, tokens), BF16),
                pltpu.VMEM((SLOTS, head_count * HDIM, tokens), BF16),
                pltpu.VMEM((head_count, tokens, 2 * HDIM), F32),
                pltpu.VMEM((head_count, tokens, 2 * HDIM), F32),
                pltpu.VMEM((3, head_count * HDIM, tokens), F32),
                dma((7,)),
                dma((SLOTS,)),
                dma((SLOTS,)),
                dma((SLOTS,)),
                dma((SLOTS,)),
                dma((heads,)),
                dma((heads,)),
                dma((SLOTS,)),
                dma((SLOTS,)),
                dma((SLOTS,)),
                dma((SLOTS,)),
                dma((SLOTS,)),
                dma((SLOTS,)),
            ],
            compiler_params=pltpu.CompilerParams(
                collective_id=0, has_side_effects=True, vmem_limit_bytes=56 * 1024 * 1024
            ),
            cost_estimate=pl.CostEstimate(flops=8 * 10**9, bytes_accessed=2 * 10**6, transcendentals=6 * 10**6),
        )(query_rows, key_rows, value_rows, attention_out, output_grad, out_weight, reach_mask)

    rows = P("seq", "head")
    return jax.shard_map(
        step,
        mesh=mesh,
        in_specs=(rows, rows, rows, rows, rows, P("head", None), P("seq", None)),
        out_specs=(rows, rows, rows),
        check_vma=False,
    )
```

```python
import jax
import jax.numpy as jnp
from jax import lax
from jax.experimental import pallas as pl
from jax.experimental.pallas import tpu as pltpu
from jax.sharding import PartitionSpec as P

MESH = pl.DeviceIdType.MESH
HDIM = 64
PLANE = 8
SLOTS = 13
DELTA = (0, -8, 8, -16, 16, -1, 1, -2, 2, -4, 4, -32, 32)
SCALING = HDIM**-0.5
EXP2_SCALE = SCALING * 1.4426950408889634
F32 = jnp.float32
BF16 = jnp.bfloat16


def mask_column(delta):
    return 2 * (abs(delta).bit_length() - 1) + (delta < 0)


def opposite(slot):
    return slot + 1 - 2 * ((slot + 1) % 2)


def slot_delta(slot):
    pair = (slot + 1) // 2
    power = (pair + 2) % 5 + 2 * (pair // 6)
    size = (1 + power % 2) * (1 + 3 * ((power // 2) % 2)) * (1 + 15 * (power // 4))
    return size * (1 - 2 * (slot % 2))


def slot_column(slot):
    pair = (slot + 1) // 2
    power = (pair + 2) % 5 + 2 * (pair // 6)
    return 2 * power + 1 - slot % 2


def turn_slot(turn, spot):
    place = turn - 5
    sign = lax.rem(place // 3 + 1 - spot // (PLANE // 2), 2)
    inner = 5 + 2 * lax.rem(place, 3) + sign
    return jnp.where(jnp.logical_and(turn >= 5, turn <= 10), inner, turn)


def dot_nt(left, right):
    return lax.dot_general(left, right, (((1,), (1,)), ((), ())), preferred_element_type=F32)


def dot_nn(left, right):
    return jnp.dot(left, right, preferred_element_type=F32)


TAIL = 16
DEAD = -1e30


def kernel(
    blocks,
    heads,
    q_hbm,
    k_hbm,
    v_hbm,
    ao_hbm,
    og_hbm,
    w_hbm,
    reach_hbm,
    dq_ref,
    dk_ref,
    dv_ref,
    k_ref,
    v_ref,
    ao_ref,
    w_ref,
    reach_ref,
    qbuf,
    gbuf,
    ogbuf,
    wide,
    ebuf,
    ubuf,
    kfull,
    vfull,
    ktrans,
    stat_out,
    stat_in,
    fact_out,
    fact_in,
    dq_raw,
    part_out,
    part_in,
    row_top,
    norm,
    dk_acc,
    dv_acc,
    local_sem,
    q_send,
    q_recv,
    g_send,
    g_recv,
    og_send,
    og_recv,
    stat_send,
    stat_recv,
    fact_send,
    fact_recv,
    part_send,
    part_recv,
):
    _, pairs, width = qbuf.shape
    head_count = width // (2 * HDIM)
    width_rows = head_count * HDIM
    me = lax.axis_index("seq")
    my_head = lax.axis_index("head")
    spot = lax.rem(me, PLANE)
    plane_start = me - spot

    def at(delta):
        return lax.rem(me + delta + blocks, blocks)

    def in_plane(delta):
        return plane_start + lax.rem(spot + delta + PLANE, PLANE)

    def stays(delta):
        return spot + delta < PLANE if delta > 0 else spot + delta >= 0

    def head_at(step):
        return lax.rem(my_head + step, heads)

    barrier = pltpu.get_barrier_semaphore()
    for delta in DELTA[1:]:
        pl.semaphore_signal(barrier, inc=1, device_id=(at(delta), my_head), device_id_type=MESH)
    for delta in (-1, 1, -2, 2, 4):
        pl.semaphore_signal(barrier, inc=1, device_id=(in_plane(delta), my_head), device_id_type=MESH)
    for step in range(1, heads):
        pl.semaphore_signal(barrier, inc=1, device_id=(me, head_at(step)), device_id_type=MESH)

    loads = [
        pltpu.make_async_copy(src, dst, local_sem.at[i])
        for i, (src, dst) in enumerate(
            [
                (k_hbm, k_ref),
                (q_hbm, qbuf.at[0]),
                (v_hbm, v_ref),
                (w_hbm, w_ref),
                (ao_hbm, ao_ref),
                (og_hbm, ogbuf.at[my_head]),
                (reach_hbm, reach_ref),
            ]
        )
    ]
    for load in loads:
        load.start()

    lane = lax.broadcasted_iota(jnp.int32, (1, 2 * HDIM), 1)
    low = lane < HDIM
    low_f = low.astype(F32)
    low_b = low_f.astype(BF16)
    high_b = (1.0 - low_f).astype(BF16)

    def cols(head):
        return pl.ds(head * 2 * HDIM, 2 * HDIM)

    def head_rows(head):
        return pl.ds(head * HDIM, HDIM)

    def doubled(tile):
        tile = tile.astype(F32)
        turned = pltpu.roll(tile, HDIM, 1)
        return jnp.concatenate([jnp.where(low, tile, turned), jnp.where(low, turned, tile)], axis=0)

    def spread(tile):
        return jnp.concatenate([tile * low_b, tile * high_b], axis=0)

    pl.semaphore_wait(barrier, 17 + heads - 1)

    def remote(src, dst, send_sem, recv_sem, seq, head=None):
        return pltpu.make_async_remote_copy(
            src_ref=src,
            dst_ref=dst,
            send_sem=send_sem,
            recv_sem=recv_sem,
            device_id=(seq, my_head if head is None else head),
            device_id_type=MESH,
        )

    queries_net = (qbuf, q_send, q_recv)
    grads_net = (gbuf, g_send, g_recv)
    stats_net = (stat_in, stat_send, stat_recv)
    facts_net = (fact_in, fact_send, fact_recv)
    parts_net = (part_in, part_send, part_recv)

    def move(net, src, dst_slot, seq):
        buf, send, recv = net
        return remote(src, buf.at[dst_slot], send.at[dst_slot], recv.at[dst_slot], seq)

    def wait_recv(net, slot):
        move(net, net[0].at[slot], slot, at(8)).wait_recv()

    def wait_send(net, slot):
        move(net, net[0].at[slot], slot, at(8)).wait_send()

    def slot_of(delta):
        return DELTA.index(delta)

    def send_own(net, src):
        for sign in (1, -1):
            move(net, src, slot_of(-8 * sign), at(8 * sign)).start()

    def send_plane_own(net, src):
        for delta in (4, -4, 2, -2, 1, -1):

            @pl.when(stays(delta))
            def _():
                move(net, src, slot_of(-delta), in_plane(delta)).start()

    def relay_near(net, sign):
        source = net[0].at[slot_of(-8 * sign)]
        move(net, source, slot_of(-16 * sign), at(8 * sign)).start()
        for size in (4, 2, 1):
            delta = size * sign

            @pl.when(jnp.logical_not(stays(delta)))
            def _():
                move(net, source, slot_of(-delta), in_plane(delta)).start()

    def relay_far(net, sign):
        move(net, net[0].at[slot_of(-16 * sign)], slot_of(-32 * sign), at(16 * sign)).start()

    send_own(queries_net, q_hbm)
    for step in range(1, heads):
        remote(og_hbm, ogbuf.at[my_head], og_send.at[step], og_recv.at[my_head], me, head_at(step)).start()
    send_plane_own(queries_net, q_hbm)

    for load in loads:
        load.wait()
    for head in range(head_count):
        keys = doubled(k_ref[:, cols(head)])
        kfull[head] = keys.astype(BF16)
        ktrans[head] = jnp.transpose(keys)[:HDIM].astype(BF16)
        vfull[head] = doubled(v_ref[:, cols(head)]).astype(BF16)
        dk_acc[head] = jnp.zeros((2 * pairs, 2 * HDIM), F32)
        dv_acc[head] = jnp.zeros((2 * pairs, 2 * HDIM), F32)
    wide[...] = jnp.zeros(wide.shape, BF16)
    for head in range(head_count):
        rows = w_ref[pl.ds(head * HDIM, HDIM), :]
        for parity in range(2):
            wide[parity, pl.ds((head * 2 + parity) * HDIM, HDIM), :] = rows

    def grads_of_attention():
        for step in range(1, heads):
            other = head_at(step)
            remote(og_hbm, ogbuf.at[other], og_send.at[step], og_recv.at[other], me, other).wait_recv()
        total = jnp.zeros((pairs, width), F32)
        for chunk in range(heads):
            half = chunk % 2
            total = total + dot_nt(ogbuf[chunk], wide[chunk // 2, :, pl.ds(half * width, width)])
        grads = total.astype(BF16)
        gbuf[0, :pairs, :] = grads
        product = grads.astype(F32) * ao_ref[...].astype(F32)
        column = lax.broadcasted_iota(jnp.int32, (1, width), 1)
        first = lax.rem(column, 2 * HDIM) < HDIM
        both = jnp.concatenate([jnp.where(first, product, 0.0), jnp.where(first, 0.0, product)], axis=0)
        top = both.astype(BF16)
        rest = (both - top.astype(F32)).astype(BF16)
        chooser = (
            lax.broadcasted_iota(jnp.int32, (8, width), 1) // (2 * HDIM)
            == lax.broadcasted_iota(jnp.int32, (8, width), 0)
        )
        chooser = chooser.astype(F32).astype(BF16)
        delta = dot_nt(chooser, top) + dot_nt(chooser, rest)
        delta_top = delta.astype(BF16)
        delta_rest = (delta - delta_top.astype(F32)).astype(BF16)
        wide_lane = lax.broadcasted_iota(jnp.int32, (1, width), 1)
        reach = jnp.zeros((1, width), F32)
        for entry in range(reach_ref.shape[1]):
            reach = jnp.where(wide_lane == entry, (reach_ref[0, entry] > 0).astype(F32), reach)
        reach = reach.astype(BF16)
        gbuf[0, pairs:, :] = jnp.concatenate([delta_top[:4], reach, delta_top[5:], delta_rest], axis=0)

    def first_pass(turn, carry):
        slot = turn_slot(turn, spot)

        @pl.when(slot > 0)
        def _():
            wait_recv(queries_net, slot)

        for sign in (1, -1):

            @pl.when(slot == slot_of(-8 * sign))
            def _():
                relay_near(queries_net, sign)

            @pl.when(slot == slot_of(-16 * sign))
            def _():
                relay_far(queries_net, sign)

        @pl.when(turn == 5)
        def _():
            grads_of_attention()
            send_own(grads_net, gbuf.at[0])
            send_plane_own(grads_net, gbuf.at[0])

        @pl.when(slot == 11)
        def _():
            for sign in (1, -1):
                wait_recv(grads_net, slot_of(-8 * sign))
                relay_near(grads_net, sign)

        tops, sums = [], []
        for head in range(head_count):
            queries = spread(qbuf[slot, :, cols(head)])
            scores = dot_nt(kfull[head], queries)
            top = jnp.max(scores, axis=0, keepdims=True)
            weights = jnp.exp2((scores - top) * EXP2_SCALE)
            tops.append(top)
            sums.append(jnp.sum(weights, axis=0, keepdims=True))
            ebuf[slot * head_count + head] = weights.astype(BF16)
        stat_out[slot] = jnp.concatenate(tops + tops[:1] + sums + sums[:1], axis=0)

        @pl.when(slot > 0)
        def _():
            there = opposite(slot)
            remote(
                stat_out.at[slot], stat_in.at[there], stat_send.at[slot], stat_recv.at[there], at(slot_delta(slot))
            ).start()

        return carry

    lax.fori_loop(0, SLOTS, first_pass, 0)

    def share_factors():
        live = [None] + [reach_ref[0, mask_column(delta)] > 0 for delta in DELTA[1:]]
        for slot in range(1, SLOTS):
            wait_recv(stats_net, slot)

        def stats(slot):
            both = stat_out[0] if slot == 0 else stat_in[slot]
            return both[0:4], both[4:8]

        highest = stats(0)[0]
        for slot in range(1, SLOTS):
            highest = jnp.maximum(highest, jnp.where(live[slot], stats(slot)[0], DEAD))
        ratios = []
        total = jnp.zeros(highest.shape, F32)
        for slot in range(SLOTS):
            top, part = stats(slot)
            if slot:
                top = jnp.where(live[slot], top, DEAD)
            ratio = jnp.exp2((top - highest) * EXP2_SCALE)
            if slot:
                ratio = jnp.where(live[slot], ratio, 0.0)
            total = total + ratio * part
            ratios.append(ratio)
        inverse = 1.0 / total
        norm[...] = jnp.concatenate([highest, inverse], axis=0)
        for slot in range(SLOTS):
            factors = ratios[slot] * inverse
            factors = jnp.concatenate([factors, factors], axis=0)
            if slot == 0:
                fact_in[0] = factors
            else:
                fact_out[slot] = factors
                there = opposite(slot)
                remote(
                    fact_out.at[slot], fact_in.at[there], fact_send.at[slot], fact_recv.at[there], at(DELTA[slot])
                ).start()

    def return_part(slot, seq):
        tops = row_top[slot]
        first = tops.astype(BF16)
        tops = tops - first.astype(F32)
        second = tops.astype(BF16)
        third = (tops - second.astype(F32)).astype(BF16)
        part_out[slot, :width_rows, :] = dq_raw[slot].astype(BF16)
        part_out[slot, width_rows:, :] = jnp.concatenate([first, second, third, third], axis=0)
        move(parts_net, part_out.at[slot], slot, seq).start()

    def merge(target, slot):
        wait_recv(parts_net, slot)
        tail = part_in[slot, width_rows:, :].astype(F32)
        theirs = tail[0:4] + tail[4:8] + tail[8:12]
        ours = row_top[target]
        top = jnp.maximum(ours, theirs)
        ours = jnp.exp2((ours - top) * EXP2_SCALE)
        theirs = jnp.exp2((theirs - top) * EXP2_SCALE)
        row_top[target] = top
        for head in range(head_count):
            rows = head_rows(head)
            one = slice(head, head + 1)
            dq_raw[target, rows, :] = dq_raw[target, rows, :] * ours[one] + part_in[slot, rows, :].astype(F32) * theirs[one]

    def second_pass(turn, carry):
        slot = turn_slot(turn, spot)

        @pl.when(slot == 3)
        def _():
            for sign in (1, -1):
                wait_recv(grads_net, slot_of(-16 * sign))
                relay_far(grads_net, sign)
            share_factors()

        @pl.when(slot > 4)
        def _():
            wait_recv(grads_net, slot)

        tail = gbuf[slot, pairs:, :].astype(F32)
        column = slot_column(slot)
        chosen = jnp.where(lax.broadcasted_iota(jnp.int32, (1, width), 1) == column, tail[4:5], 0.0)
        alive = jnp.maximum(jnp.sum(chosen, axis=1, keepdims=True), (slot == 0).astype(F32))
        row_top[slot] = jnp.where(alive > 0.5, stat_out[slot, 0:4, :], DEAD)
        for head in range(head_count):
            grads = spread(gbuf[slot, :pairs, cols(head)])
            shift = tail[head : head + 1] + tail[8 + head : 9 + head]
            prob_grad = dot_nt(vfull[head], grads)
            weights = ebuf[slot * head_count + head].astype(F32)
            raw = (weights * (prob_grad - shift)).astype(BF16)
            ubuf[slot * head_count + head] = raw
            dq_raw[slot, head_rows(head), :] = dot_nn(ktrans[head], raw) * alive

        @pl.when(jnp.logical_and(slot > 4, slot < 11))
        def _():
            return_part(slot, in_plane(slot_delta(slot)))

        @pl.when(slot == slot_of(-32))
        def _():
            return_part(slot_of(-32), at(-16))

        @pl.when(slot == slot_of(32))
        def _():
            return_part(slot_of(32), at(16))

        return carry

    lax.fori_loop(0, SLOTS, second_pass, 0)

    for sign in (1, -1):
        near = slot_of(-16 * sign)
        merge(near, slot_of(-32 * sign))
        return_part(near, at(-8 * sign))

    def third_pass(slot, carry):
        @pl.when(slot > 0)
        def _():
            wait_recv(facts_net, slot)

        factors = fact_in[slot]
        for head in range(head_count):
            factor = factors[head : head + 1]
            queries = spread(qbuf[slot, :, cols(head)])
            grads = spread(gbuf[slot, :pairs, cols(head)])
            prob = (ebuf[slot * head_count + head].astype(F32) * factor).astype(BF16)
            score_grad = (ubuf[slot * head_count + head].astype(F32) * factor).astype(BF16)
            dv_acc[head] += dot_nn(prob, grads)
            dk_acc[head] += dot_nn(score_grad, queries)

        @pl.when(slot == 6)
        def _():
            for delta in (2, -2, 4, -4, 1, -1):
                owner = jnp.where(stays(delta), 0, slot_of(-8) if delta > 0 else slot_of(8))
                merge(owner, slot_of(-delta))
            for sign in (1, -1):
                next_to = slot_of(-8 * sign)
                merge(next_to, slot_of(-16 * sign))
                return_part(next_to, at(-8 * sign))

        return carry

    lax.fori_loop(0, SLOTS, third_pass, 0)

    def folded(wide_sum):
        both = wide_sum + pltpu.roll(wide_sum, HDIM, 1)
        return jnp.where(low, both[:pairs], both[pairs:])

    for head in range(head_count):
        dk_ref[:, cols(head)] = (folded(dk_acc[head]) * SCALING).astype(BF16)
        dv_ref[:, cols(head)] = folded(dv_acc[head]).astype(BF16)

    for sign in (1, -1):
        merge(0, slot_of(-8 * sign))
    final = jnp.exp2((row_top[0] - norm[0:4]) * EXP2_SCALE) * norm[4:8] * SCALING
    for head in range(head_count):
        rows = dq_raw[0, head_rows(head), :] * final[head : head + 1]
        turned = jnp.transpose(jnp.concatenate([rows, rows], axis=0))
        dq_ref[:, cols(head)] = jnp.where(low, turned[:pairs], turned[pairs:]).astype(BF16)

    for step in range(1, heads):
        remote(og_hbm, ogbuf.at[my_head], og_send.at[step], og_recv.at[my_head], me, head_at(step)).wait_send()

    def drain(slot, carry):
        for net in (queries_net, grads_net, stats_net, facts_net, parts_net):
            wait_send(net, slot)
        return carry

    lax.fori_loop(1, SLOTS, drain, 0)


def solution(mesh):
    blocks, heads = mesh.shape["seq"], mesh.shape["head"]

    def step(query_rows, key_rows, value_rows, attention_out, output_grad, out_weight, reach_mask):
        pairs, width = query_rows.shape
        head_count = width // (2 * HDIM)
        tokens = 2 * pairs
        vmem = pl.BlockSpec(memory_space=pltpu.VMEM)
        block = jax.ShapeDtypeStruct((pairs, width), BF16)
        dma = pltpu.SemaphoreType.DMA

        def body(*refs):
            kernel(blocks, heads, *refs)

        return pl.pallas_call(
            body,
            out_shape=(block, block, block),
            in_specs=[pl.BlockSpec(memory_space=pltpu.HBM)] * 7,
            out_specs=(vmem, vmem, vmem),
            scratch_shapes=[
                pltpu.VMEM((pairs, width), BF16),
                pltpu.VMEM((pairs, width), BF16),
                pltpu.VMEM((pairs, width), BF16),
                pltpu.VMEM(out_weight.shape, BF16),
                pltpu.SMEM(reach_mask.shape, jnp.int32),
                pltpu.VMEM((SLOTS, pairs, width), BF16),
                pltpu.VMEM((SLOTS, pairs + TAIL, width), BF16),
                pltpu.VMEM((heads, pairs, width), BF16),
                pltpu.VMEM((2, width, out_weight.shape[1]), BF16),
                pltpu.VMEM((SLOTS * head_count, tokens, tokens), BF16),
                pltpu.VMEM((SLOTS * head_count, tokens, tokens), BF16),
                pltpu.VMEM((head_count, tokens, 2 * HDIM), BF16),
                pltpu.VMEM((head_count, tokens, 2 * HDIM), BF16),
                pltpu.VMEM((head_count, HDIM, tokens), BF16),
                pltpu.VMEM((SLOTS, 8, tokens), F32),
                pltpu.VMEM((SLOTS, 8, tokens), F32),
                pltpu.VMEM((SLOTS, 8, tokens), F32),
                pltpu.VMEM((SLOTS, 8, tokens), F32),
                pltpu.VMEM((SLOTS, head_count * HDIM, tokens), F32),
                pltpu.VMEM((SLOTS, head_count * HDIM + TAIL, tokens), BF16),
                pltpu.VMEM((SLOTS, head_count * HDIM + TAIL, tokens), BF16),
                pltpu.VMEM((SLOTS, 4, tokens), F32),
                pltpu.VMEM((8, tokens), F32),
                pltpu.VMEM((head_count, tokens, 2 * HDIM), F32),
                pltpu.VMEM((head_count, tokens, 2 * HDIM), F32),
                dma((7,)),
                dma((SLOTS,)),
                dma((SLOTS,)),
                dma((SLOTS,)),
                dma((SLOTS,)),
                dma((heads,)),
                dma((heads,)),
                dma((SLOTS,)),
                dma((SLOTS,)),
                dma((SLOTS,)),
                dma((SLOTS,)),
                dma((SLOTS,)),
                dma((SLOTS,)),
            ],
            compiler_params=pltpu.CompilerParams(
                collective_id=0, has_side_effects=True, vmem_limit_bytes=56 * 1024 * 1024
            ),
            cost_estimate=pl.CostEstimate(flops=8 * 10**9, bytes_accessed=2 * 10**6, transcendentals=6 * 10**6),
        )(query_rows, key_rows, value_rows, attention_out, output_grad, out_weight, reach_mask)

    rows = P("seq", "head")
    return jax.shard_map(
        step,
        mesh=mesh,
        in_specs=(rows, rows, rows, rows, rows, P("head", None), P("seq", None)),
        out_specs=(rows, rows, rows),
        check_vma=False,
    )
```

```python
import jax
import jax.numpy as jnp
from jax import lax
from jax.experimental import pallas as pl
from jax.experimental.pallas import tpu as pltpu
from jax.sharding import PartitionSpec as P

MESH = pl.DeviceIdType.MESH
HDIM = 64
PLANE = 8
SLOTS = 13
DELTA = (0, -8, 8, -16, 16, -1, 1, -2, 2, -4, 4, -32, 32)
SCALING = HDIM**-0.5
EXP2_SCALE = SCALING * 1.4426950408889634
F32 = jnp.float32
BF16 = jnp.bfloat16


def mask_column(delta):
    return 2 * (abs(delta).bit_length() - 1) + (delta < 0)


def opposite(slot):
    return slot + 1 - 2 * ((slot + 1) % 2)


def slot_delta(slot):
    pair = (slot + 1) // 2
    power = (pair + 2) % 5 + 2 * (pair // 6)
    size = (1 + power % 2) * (1 + 3 * ((power // 2) % 2)) * (1 + 15 * (power // 4))
    return size * (1 - 2 * (slot % 2))


def slot_column(slot):
    pair = (slot + 1) // 2
    power = (pair + 2) % 5 + 2 * (pair // 6)
    return 2 * power + 1 - slot % 2


def turn_slot(turn, spot):
    place = turn - 5
    sign = lax.rem(place // 3 + 1 - spot // (PLANE // 2), 2)
    inner = 5 + 2 * lax.rem(place, 3) + sign
    return jnp.where(jnp.logical_and(turn >= 5, turn <= 10), inner, turn)


def dot_nt(left, right):
    return lax.dot_general(left, right, (((1,), (1,)), ((), ())), preferred_element_type=F32)


def dot_nn(left, right):
    return jnp.dot(left, right, preferred_element_type=F32)


TAIL = 16
DEAD = -1e30


def kernel(
    blocks,
    heads,
    q_hbm,
    k_hbm,
    v_hbm,
    ao_hbm,
    og_hbm,
    w_hbm,
    reach_hbm,
    dq_ref,
    dk_ref,
    dv_ref,
    k_ref,
    v_ref,
    ao_ref,
    w_ref,
    reach_ref,
    qbuf,
    gbuf,
    ogbuf,
    wide,
    ebuf,
    ubuf,
    kfull,
    vfull,
    ktrans,
    stat_out,
    stat_in,
    fact_out,
    fact_in,
    dq_raw,
    part_out,
    part_in,
    row_top,
    norm,
    dk_acc,
    dv_acc,
    local_sem,
    q_send,
    q_recv,
    g_send,
    g_recv,
    og_send,
    og_recv,
    stat_send,
    stat_recv,
    fact_send,
    fact_recv,
    part_send,
    part_recv,
):
    _, pairs, width = qbuf.shape
    head_count = width // (2 * HDIM)
    width_rows = head_count * HDIM
    me = lax.axis_index("seq")
    my_head = lax.axis_index("head")
    spot = lax.rem(me, PLANE)
    plane_start = me - spot

    def at(delta):
        return lax.rem(me + delta + blocks, blocks)

    def in_plane(delta):
        return plane_start + lax.rem(spot + delta + PLANE, PLANE)

    def stays(delta):
        return spot + delta < PLANE if delta > 0 else spot + delta >= 0

    def head_at(step):
        return lax.rem(my_head + step, heads)

    barrier = pltpu.get_barrier_semaphore()
    for delta in DELTA[1:]:
        pl.semaphore_signal(barrier, inc=1, device_id=(at(delta), my_head), device_id_type=MESH)
    for delta in (-1, 1, -2, 2, 4):
        pl.semaphore_signal(barrier, inc=1, device_id=(in_plane(delta), my_head), device_id_type=MESH)
    for step in range(1, heads):
        pl.semaphore_signal(barrier, inc=1, device_id=(me, head_at(step)), device_id_type=MESH)

    loads = [
        pltpu.make_async_copy(src, dst, local_sem.at[i])
        for i, (src, dst) in enumerate(
            [
                (k_hbm, k_ref),
                (q_hbm, qbuf.at[0]),
                (v_hbm, v_ref),
                (w_hbm, w_ref),
                (ao_hbm, ao_ref),
                (og_hbm, ogbuf.at[my_head]),
                (reach_hbm, reach_ref),
            ]
        )
    ]
    for load in loads:
        load.start()

    lane = lax.broadcasted_iota(jnp.int32, (1, 2 * HDIM), 1)
    low = lane < HDIM
    low_f = low.astype(F32)
    low_b = low_f.astype(BF16)
    high_b = (1.0 - low_f).astype(BF16)

    def cols(head):
        return pl.ds(head * 2 * HDIM, 2 * HDIM)

    def head_rows(head):
        return pl.ds(head * HDIM, HDIM)

    def doubled(tile):
        tile = tile.astype(F32)
        turned = pltpu.roll(tile, HDIM, 1)
        return jnp.concatenate([jnp.where(low, tile, turned), jnp.where(low, turned, tile)], axis=0)

    def spread(tile):
        return jnp.concatenate([tile * low_b, tile * high_b], axis=0)

    pl.semaphore_wait(barrier, 17 + heads - 1)

    def remote(src, dst, send_sem, recv_sem, seq, head=None):
        return pltpu.make_async_remote_copy(
            src_ref=src,
            dst_ref=dst,
            send_sem=send_sem,
            recv_sem=recv_sem,
            device_id=(seq, my_head if head is None else head),
            device_id_type=MESH,
        )

    queries_net = (qbuf, q_send, q_recv)
    grads_net = (gbuf, g_send, g_recv)
    stats_net = (stat_in, stat_send, stat_recv)
    facts_net = (fact_in, fact_send, fact_recv)
    parts_net = (part_in, part_send, part_recv)

    def move(net, src, dst_slot, seq):
        buf, send, recv = net
        return remote(src, buf.at[dst_slot], send.at[dst_slot], recv.at[dst_slot], seq)

    def wait_recv(net, slot):
        move(net, net[0].at[slot], slot, at(8)).wait_recv()

    def wait_send(net, slot):
        move(net, net[0].at[slot], slot, at(8)).wait_send()

    def slot_of(delta):
        return DELTA.index(delta)

    def send_own(net, src):
        for sign in (1, -1):
            move(net, src, slot_of(-8 * sign), at(8 * sign)).start()

    def send_plane_own(net, src):
        for delta in (4, -4, 2, -2, 1, -1):

            @pl.when(stays(delta))
            def _():
                move(net, src, slot_of(-delta), in_plane(delta)).start()

    def relay_near(net, sign):
        source = net[0].at[slot_of(-8 * sign)]
        move(net, source, slot_of(-16 * sign), at(8 * sign)).start()
        for size in (4, 2, 1):
            delta = size * sign

            @pl.when(jnp.logical_not(stays(delta)))
            def _():
                move(net, source, slot_of(-delta), in_plane(delta)).start()

    def relay_far(net, sign):
        move(net, net[0].at[slot_of(-16 * sign)], slot_of(-32 * sign), at(16 * sign)).start()

    send_own(queries_net, q_hbm)
    for step in range(1, heads):
        remote(og_hbm, ogbuf.at[my_head], og_send.at[step], og_recv.at[my_head], me, head_at(step)).start()
    send_plane_own(queries_net, q_hbm)

    for load in loads:
        load.wait()
    for head in range(head_count):
        keys = doubled(k_ref[:, cols(head)])
        kfull[head] = keys.astype(BF16)
        ktrans[head] = jnp.transpose(keys)[:HDIM].astype(BF16)
        vfull[head] = doubled(v_ref[:, cols(head)]).astype(BF16)
        dk_acc[head] = jnp.zeros((2 * pairs, 2 * HDIM), F32)
        dv_acc[head] = jnp.zeros((2 * pairs, 2 * HDIM), F32)
    wide[...] = jnp.zeros(wide.shape, BF16)
    for head in range(head_count):
        rows = w_ref[pl.ds(head * HDIM, HDIM), :]
        for parity in range(2):
            wide[parity, pl.ds((head * 2 + parity) * HDIM, HDIM), :] = rows

    def grads_of_attention():
        for step in range(1, heads):
            other = head_at(step)
            remote(og_hbm, ogbuf.at[other], og_send.at[step], og_recv.at[other], me, other).wait_recv()
        total = jnp.zeros((pairs, width), F32)
        for chunk in range(heads):
            half = chunk % 2
            total = total + dot_nt(ogbuf[chunk], wide[chunk // 2, :, pl.ds(half * width, width)])
        grads = total.astype(BF16)
        gbuf[0, :pairs, :] = grads
        product = grads.astype(F32) * ao_ref[...].astype(F32)
        column = lax.broadcasted_iota(jnp.int32, (1, width), 1)
        first = lax.rem(column, 2 * HDIM) < HDIM
        both = jnp.concatenate([jnp.where(first, product, 0.0), jnp.where(first, 0.0, product)], axis=0)
        top = both.astype(BF16)
        rest = (both - top.astype(F32)).astype(BF16)
        chooser = (
            lax.broadcasted_iota(jnp.int32, (8, width), 1) // (2 * HDIM)
            == lax.broadcasted_iota(jnp.int32, (8, width), 0)
        )
        chooser = chooser.astype(F32).astype(BF16)
        delta = dot_nt(chooser, top) + dot_nt(chooser, rest)
        delta_top = delta.astype(BF16)
        delta_rest = (delta - delta_top.astype(F32)).astype(BF16)
        wide_lane = lax.broadcasted_iota(jnp.int32, (1, width), 1)
        reach = jnp.zeros((1, width), F32)
        for entry in range(reach_ref.shape[1]):
            reach = jnp.where(wide_lane == entry, (reach_ref[0, entry] > 0).astype(F32), reach)
        reach = reach.astype(BF16)
        gbuf[0, pairs:, :] = jnp.concatenate([delta_top[:4], reach, delta_top[5:], delta_rest], axis=0)

    def first_pass(turn, carry):
        slot = turn_slot(turn, spot)

        @pl.when(slot > 0)
        def _():
            wait_recv(queries_net, slot)

        for sign in (1, -1):

            @pl.when(slot == slot_of(-8 * sign))
            def _():
                relay_near(queries_net, sign)

            @pl.when(slot == slot_of(-16 * sign))
            def _():
                relay_far(queries_net, sign)

        @pl.when(turn == 5)
        def _():
            grads_of_attention()
            send_own(grads_net, gbuf.at[0])
            send_plane_own(grads_net, gbuf.at[0])

        @pl.when(slot == 11)
        def _():
            for sign in (1, -1):
                wait_recv(grads_net, slot_of(-8 * sign))
                relay_near(grads_net, sign)

        tops, sums = [], []
        for head in range(head_count):
            queries = spread(qbuf[slot, :, cols(head)])
            scores = dot_nt(kfull[head], queries)
            top = jnp.max(scores, axis=0, keepdims=True)
            weights = jnp.exp2((scores - top) * EXP2_SCALE)
            tops.append(top)
            sums.append(jnp.sum(weights, axis=0, keepdims=True))
            ebuf[slot * head_count + head] = weights.astype(BF16)
        stat_out[slot] = jnp.concatenate(tops + tops[:1] + sums + sums[:1], axis=0)

        @pl.when(slot > 0)
        def _():
            there = opposite(slot)
            remote(
                stat_out.at[slot], stat_in.at[there], stat_send.at[slot], stat_recv.at[there], at(slot_delta(slot))
            ).start()

        return carry

    lax.fori_loop(0, SLOTS, first_pass, 0)

    def share_factors():
        live = [None] + [reach_ref[0, mask_column(delta)] > 0 for delta in DELTA[1:]]
        for slot in range(1, SLOTS):
            wait_recv(stats_net, slot)

        def stats(slot):
            both = stat_out[0] if slot == 0 else stat_in[slot]
            return both[0:4], both[4:8]

        highest = stats(0)[0]
        for slot in range(1, SLOTS):
            highest = jnp.maximum(highest, jnp.where(live[slot], stats(slot)[0], DEAD))
        ratios = []
        total = jnp.zeros(highest.shape, F32)
        for slot in range(SLOTS):
            top, part = stats(slot)
            if slot:
                top = jnp.where(live[slot], top, DEAD)
            ratio = jnp.exp2((top - highest) * EXP2_SCALE)
            if slot:
                ratio = jnp.where(live[slot], ratio, 0.0)
            total = total + ratio * part
            ratios.append(ratio)
        inverse = 1.0 / total
        norm[...] = jnp.concatenate([highest, inverse], axis=0)
        for slot in range(SLOTS):
            factors = ratios[slot] * inverse
            factors = jnp.concatenate([factors, factors], axis=0)
            if slot == 0:
                fact_in[0] = factors
            else:
                fact_out[slot] = factors
                there = opposite(slot)
                remote(
                    fact_out.at[slot], fact_in.at[there], fact_send.at[slot], fact_recv.at[there], at(DELTA[slot])
                ).start()

    def return_part(slot, seq):
        tops = row_top[slot]
        first = tops.astype(BF16)
        tops = tops - first.astype(F32)
        second = tops.astype(BF16)
        third = (tops - second.astype(F32)).astype(BF16)
        part_out[slot, :width_rows, :] = dq_raw[slot].astype(BF16)
        part_out[slot, width_rows:, :] = jnp.concatenate([first, second, third, third], axis=0)
        move(parts_net, part_out.at[slot], slot, seq).start()

    def merge(target, slot):
        wait_recv(parts_net, slot)
        tail = part_in[slot, width_rows:, :].astype(F32)
        theirs = tail[0:4] + tail[4:8] + tail[8:12]
        ours = row_top[target]
        top = jnp.maximum(ours, theirs)
        ours = jnp.exp2((ours - top) * EXP2_SCALE)
        theirs = jnp.exp2((theirs - top) * EXP2_SCALE)
        row_top[target] = top
        for head in range(head_count):
            rows = head_rows(head)
            one = slice(head, head + 1)
            dq_raw[target, rows, :] = dq_raw[target, rows, :] * ours[one] + part_in[slot, rows, :].astype(F32) * theirs[one]

    def second_pass(turn, carry):
        slot = turn_slot(turn, spot)

        @pl.when(slot == 3)
        def _():
            for sign in (1, -1):
                wait_recv(grads_net, slot_of(-16 * sign))
                relay_far(grads_net, sign)
            share_factors()

        @pl.when(slot > 4)
        def _():
            wait_recv(grads_net, slot)

        tail = gbuf[slot, pairs:, :].astype(F32)
        column = slot_column(slot)
        chosen = jnp.where(lax.broadcasted_iota(jnp.int32, (1, width), 1) == column, tail[4:5], 0.0)
        alive = jnp.maximum(jnp.sum(chosen, axis=1, keepdims=True), (slot == 0).astype(F32))
        row_top[slot] = jnp.where(alive > 0.5, stat_out[slot, 0:4, :], DEAD)
        for head in range(head_count):
            grads = spread(gbuf[slot, :pairs, cols(head)])
            shift = tail[head : head + 1] + tail[8 + head : 9 + head]
            prob_grad = dot_nt(vfull[head], grads)
            weights = ebuf[slot * head_count + head].astype(F32)
            raw = (weights * (prob_grad - shift)).astype(BF16)
            ubuf[slot * head_count + head] = raw
            dq_raw[slot, head_rows(head), :] = dot_nn(ktrans[head], raw) * alive

        @pl.when(jnp.logical_and(slot > 4, slot < 11))
        def _():
            return_part(slot, in_plane(slot_delta(slot)))

        @pl.when(slot == slot_of(-32))
        def _():
            return_part(slot_of(-32), at(-16))

        @pl.when(slot == slot_of(32))
        def _():
            return_part(slot_of(32), at(16))

        return carry

    lax.fori_loop(0, SLOTS, second_pass, 0)

    for sign in (1, -1):
        near = slot_of(-16 * sign)
        merge(near, slot_of(-32 * sign))
        return_part(near, at(-8 * sign))

    def third_pass(slot, carry):
        @pl.when(slot > 0)
        def _():
            wait_recv(facts_net, slot)

        factors = fact_in[slot]
        for head in range(head_count):
            factor = factors[head : head + 1]
            queries = spread(qbuf[slot, :, cols(head)])
            grads = spread(gbuf[slot, :pairs, cols(head)])
            prob = (ebuf[slot * head_count + head].astype(F32) * factor).astype(BF16)
            score_grad = (ubuf[slot * head_count + head].astype(F32) * factor).astype(BF16)
            dv_acc[head] += dot_nn(prob, grads)
            dk_acc[head] += dot_nn(score_grad, queries)

        @pl.when(slot == 6)
        def _():
            for delta in (2, -2, 4, -4, 1, -1):

                @pl.when(jnp.logical_not(stays(delta)))
                def _():
                    merge(slot_of(-8) if delta > 0 else slot_of(8), slot_of(-delta))

            for sign in (1, -1):
                next_to = slot_of(-8 * sign)
                merge(next_to, slot_of(-16 * sign))
                return_part(next_to, at(-8 * sign))

        return carry

    lax.fori_loop(0, SLOTS, third_pass, 0)

    def folded(wide_sum):
        both = wide_sum + pltpu.roll(wide_sum, HDIM, 1)
        return jnp.where(low, both[:pairs], both[pairs:])

    for head in range(head_count):
        dk_ref[:, cols(head)] = (folded(dk_acc[head]) * SCALING).astype(BF16)
        dv_ref[:, cols(head)] = folded(dv_acc[head]).astype(BF16)

    for delta in (2, -2, 4, -4, 1, -1):

        @pl.when(stays(delta))
        def _():
            merge(0, slot_of(-delta))

    for sign in (1, -1):
        merge(0, slot_of(-8 * sign))
    final = jnp.exp2((row_top[0] - norm[0:4]) * EXP2_SCALE) * norm[4:8] * SCALING
    for head in range(head_count):
        rows = dq_raw[0, head_rows(head), :] * final[head : head + 1]
        turned = jnp.transpose(jnp.concatenate([rows, rows], axis=0))
        dq_ref[:, cols(head)] = jnp.where(low, turned[:pairs], turned[pairs:]).astype(BF16)

    for step in range(1, heads):
        remote(og_hbm, ogbuf.at[my_head], og_send.at[step], og_recv.at[my_head], me, head_at(step)).wait_send()

    def drain(slot, carry):
        for net in (queries_net, grads_net, stats_net, facts_net, parts_net):
            wait_send(net, slot)
        return carry

    lax.fori_loop(1, SLOTS, drain, 0)


def solution(mesh):
    blocks, heads = mesh.shape["seq"], mesh.shape["head"]

    def step(query_rows, key_rows, value_rows, attention_out, output_grad, out_weight, reach_mask):
        pairs, width = query_rows.shape
        head_count = width // (2 * HDIM)
        tokens = 2 * pairs
        vmem = pl.BlockSpec(memory_space=pltpu.VMEM)
        block = jax.ShapeDtypeStruct((pairs, width), BF16)
        dma = pltpu.SemaphoreType.DMA

        def body(*refs):
            kernel(blocks, heads, *refs)

        return pl.pallas_call(
            body,
            out_shape=(block, block, block),
            in_specs=[pl.BlockSpec(memory_space=pltpu.HBM)] * 7,
            out_specs=(vmem, vmem, vmem),
            scratch_shapes=[
                pltpu.VMEM((pairs, width), BF16),
                pltpu.VMEM((pairs, width), BF16),
                pltpu.VMEM((pairs, width), BF16),
                pltpu.VMEM(out_weight.shape, BF16),
                pltpu.SMEM(reach_mask.shape, jnp.int32),
                pltpu.VMEM((SLOTS, pairs, width), BF16),
                pltpu.VMEM((SLOTS, pairs + TAIL, width), BF16),
                pltpu.VMEM((heads, pairs, width), BF16),
                pltpu.VMEM((2, width, out_weight.shape[1]), BF16),
                pltpu.VMEM((SLOTS * head_count, tokens, tokens), BF16),
                pltpu.VMEM((SLOTS * head_count, tokens, tokens), BF16),
                pltpu.VMEM((head_count, tokens, 2 * HDIM), BF16),
                pltpu.VMEM((head_count, tokens, 2 * HDIM), BF16),
                pltpu.VMEM((head_count, HDIM, tokens), BF16),
                pltpu.VMEM((SLOTS, 8, tokens), F32),
                pltpu.VMEM((SLOTS, 8, tokens), F32),
                pltpu.VMEM((SLOTS, 8, tokens), F32),
                pltpu.VMEM((SLOTS, 8, tokens), F32),
                pltpu.VMEM((SLOTS, head_count * HDIM, tokens), F32),
                pltpu.VMEM((SLOTS, head_count * HDIM + TAIL, tokens), BF16),
                pltpu.VMEM((SLOTS, head_count * HDIM + TAIL, tokens), BF16),
                pltpu.VMEM((SLOTS, 4, tokens), F32),
                pltpu.VMEM((8, tokens), F32),
                pltpu.VMEM((head_count, tokens, 2 * HDIM), F32),
                pltpu.VMEM((head_count, tokens, 2 * HDIM), F32),
                dma((7,)),
                dma((SLOTS,)),
                dma((SLOTS,)),
                dma((SLOTS,)),
                dma((SLOTS,)),
                dma((heads,)),
                dma((heads,)),
                dma((SLOTS,)),
                dma((SLOTS,)),
                dma((SLOTS,)),
                dma((SLOTS,)),
                dma((SLOTS,)),
                dma((SLOTS,)),
            ],
            compiler_params=pltpu.CompilerParams(
                collective_id=0, has_side_effects=True, vmem_limit_bytes=56 * 1024 * 1024
            ),
            cost_estimate=pl.CostEstimate(flops=8 * 10**9, bytes_accessed=2 * 10**6, transcendentals=6 * 10**6),
        )(query_rows, key_rows, value_rows, attention_out, output_grad, out_weight, reach_mask)

    rows = P("seq", "head")
    return jax.shard_map(
        step,
        mesh=mesh,
        in_specs=(rows, rows, rows, rows, rows, P("head", None), P("seq", None)),
        out_specs=(rows, rows, rows),
        check_vma=False,
    )
```
